32 devices in a mesh: groups: 2 (over x), rows: 16 (over z, y, core).
Axes of the slice: x: 2, y: 2, z: 4, core: 2. Of those that a mesh axis runs over, the one named last changes fastest.
Arguments:
- potential: float32 [256, 256], P(('groups', 'rows')), parts along dimension 0, may hold values from -4 to 6
- near_tiles: bfloat16 [512, 256, 256], P(('groups', 'rows')), parts along dimension 0, may hold values from -1 to 1.25
- far_left: bfloat16 [1536, 64, 256], P(('groups', 'rows')), parts along dimension 0, may hold values from -1 to 1.25
- far_right: bfloat16 [1536, 64, 256], P(('groups', 'rows')), parts along dimension 0, may hold values from -1 to 1.25
- col_owner: int32 [2048, 1], P(('groups', 'rows')), parts along dimension 0, may hold values from 0 to 15; in each aligned block of 64 rows (0 to 63, 64 to 127, ...) at most 8 rows name the same one
- col_local: int32 [2048], P(('groups', 'rows')), parts along dimension 0, may hold values from 0 to 7
- row_owner: int32 [2048, 1], P(('groups', 'rows')), parts along dimension 0, may hold values from 0 to 15; in each aligned block of 64 rows (0 to 63, 64 to 127, ...) at most 8 rows name the same one
- row_local: int32 [2048], P(('groups', 'rows')), parts along dimension 0, may hold values from 0 to 7
- far_rank: int32 [1536], P(('groups', 'rows')), parts along dimension 0, may hold values from 8 to 64
Outputs:
- krylov: float32 [2, 256, 256], P(None, ('groups', 'rows')), parts along dimension 1
- hessen: float32 [2, 6], P('groups'), parts along dimension 0
The draws below stay inside these ranges and needn't reach their ends.
There are 2 independent parts, one for each index of `groups`. The reference program is written for one: setup_inputs(seed, part) draws one part's arguments, and reference() takes and returns one part's arrays. A program takes and returns all parts, laid end to end along the dimension named above; each array names one. Nothing has to cross between parts.
Inputs may be any that keep to these rules, and one draw needn't show every extreme that they name: `col_owner`: among the blocks of one index of rows at most 8 name the same column owner, a bound that some block reaches. `row_owner`: among the blocks of one index of rows at most 8 name the same row owner, a bound that some block reaches.
All inputs are finite; a program needn't handle non-finite values.
Results may differ from the reference program's by a relative error of at most 0.0023.
Values may be sent and summed in bfloat16 or wider, within the bound.
A program may use at most 64 MiB of HBM per device.

```python
import math
import jax
import jax.numpy as jnp
import numpy as np
from jax import lax

LEAF = 256
RMAX = 64
C_DEV = 8
NEAR_DEV = 16
FAR_DEV = 48
BLK_DEV = 64
CAP = 8
NCL = 128
PANELS = 32768
BLOCKS = 1024
NEAR_TOT = 256
FAR_TOT = 768
N_ROWS = 16


def lifted(noise, fan, lift):
    return (noise + lift * fan ** (-0.5)) * fan ** (-0.5)


def draw_potential(key, part):
    key = jax.random.fold_in(key, 11)
    noise = jnp.clip(jax.random.normal(key, (NCL, LEAF), jnp.float32), -5.0, 5.0)
    return (1.0 + noise).astype(jnp.float32)


def draw_near_tiles(key, part):
    key = jax.random.fold_in(key, 21)
    shape = (NEAR_TOT, LEAF, LEAF)
    noise = jnp.clip(jax.random.normal(key, shape, jnp.float32), -4.0, 4.0)
    return lifted(noise, LEAF, 2.0).astype(jnp.bfloat16)


def draw_far_left(key, part):
    key = jax.random.fold_in(key, 31)
    shape = (FAR_TOT, RMAX, LEAF)
    noise = jnp.clip(jax.random.normal(key, shape, jnp.float32), -4.0, 4.0)
    return lifted(noise, RMAX, 2.0).astype(jnp.bfloat16)


def draw_far_right(key, part):
    key = jax.random.fold_in(key, 41)
    shape = (FAR_TOT, RMAX, LEAF)
    noise = jnp.clip(jax.random.normal(key, shape, jnp.float32), -4.0, 4.0)
    return lifted(noise, LEAF, 2.0).astype(jnp.bfloat16)


def set_ends(result, rng, low, high):
    extent = result.shape
    place = [jax.random.randint(jax.random.fold_in(rng, axis), (), 0, extent[axis]) for axis in range(len(extent))]
    result = result.at[tuple(place)].set(low)
    longest = extent.index(max(extent))
    place[longest] = (place[longest] + 1) % extent[longest]
    return result.at[tuple(place)].set(high)


def assign_block(rng, own, number, rows, count, top, most, slope):
    ranking = jax.random.permutation(rng, count)
    crowded, usual = load_shares(count, rows * top, most, slope, True), load_shares(count, rows * top, most, slope, False)
    places = jnp.arange(count)

    def named(tallies, rotation):
        used = int((tallies > 0).sum())
        fixed = max(1, used // 4)
        passed = fixed + (places - fixed + rotation * (used - fixed)) % max(1, count - fixed)
        return jnp.zeros((count,), jnp.int32).at[ranking[jnp.where(places < fixed, places, passed)]].set(jnp.asarray(tallies, jnp.int32))

    tallies = jnp.where(number % 4 == 0, named(crowded, number // 4), named(usual, number - number // 4 - 1))
    mixed = jax.random.permutation(jax.random.fold_in(own, 3), count)
    giver, receiver = mixed[0:count // 2 * 2:2], mixed[1:count // 2 * 2:2]
    room = jnp.minimum(tallies[giver] - 1, most - tallies[receiver]) // 2
    room = jnp.where((giver == ranking[0]) | (receiver == ranking[0]) | (tallies[receiver] == 0), 0, jnp.maximum(room, 0))
    passed = jax.random.randint(jax.random.fold_in(own, 4), (count // 2,), 0, 1 << 20) % (room + 1)
    tallies = tallies.at[giver].add(-passed).at[receiver].add(passed)
    members = jnp.searchsorted(jnp.cumsum(tallies), jnp.arange(rows * top), side="right").astype(jnp.int32)
    table = members.reshape(top, rows).T
    table = table[jax.random.permutation(jax.random.fold_in(own, 1), rows)]
    rotation = jax.random.randint(jax.random.fold_in(own, 2), (rows, 1), 0, top)
    return jnp.take_along_axis(table, (jnp.arange(top)[None, :] + rotation) % top, axis=1)


def load_shares(number_of, total, most, slope, full):
    weights = [(1 << 20) // math.isqrt(standing ** slope) + 1 for standing in range(1, number_of + 1)]
    largest = most if full else min(most, max(-(-total // number_of), total * weights[0] // sum(weights)))
    least = 1 if total - largest >= number_of - 1 else 0
    given, spare = [largest] + [least] * (number_of - 1), total - largest - least * (number_of - 1)
    while spare > 0:
        candidates = [i for i in range(1, number_of) if given[i] < largest] or [i for i in range(1, number_of) if given[i] < most]
        mass, budget = sum([weights[i] for i in candidates]), spare
        for i in candidates:
            extra = min(most - given[i], max(1, budget * weights[i] // mass), spare)
            given[i] = given[i] + extra
            spare = spare - extra
    return np.array(given)


def setup_inputs(seed: int = 0, part: int = 0) -> dict:
    arg_keys = jax.random.split(jax.random.key(seed), 10)
    part_keys = jax.random.split(jax.random.fold_in(arg_keys[9], part), 10)
    potential = draw_potential(jax.random.fold_in(jax.random.fold_in(arg_keys[9], part), 71), part)
    near_tiles = draw_near_tiles(jax.random.fold_in(jax.random.fold_in(arg_keys[9], part), 71), part)
    far_left = draw_far_left(jax.random.fold_in(jax.random.fold_in(arg_keys[9], part), 71), part)
    far_right = draw_far_right(jax.random.fold_in(jax.random.fold_in(arg_keys[9], part), 71), part)
    col_owner_keys = jax.random.split(jax.random.fold_in(part_keys[4], 1), BLOCKS // BLK_DEV)
    col_owner_turns = jax.random.permutation(jax.random.fold_in(part_keys[4], 3), BLOCKS // BLK_DEV)
    col_owner = jax.vmap(lambda own, number: assign_block(jax.random.fold_in(part_keys[4], 2), own, number, BLK_DEV, N_ROWS, 1, CAP, 2))(col_owner_keys, col_owner_turns).reshape((BLOCKS, 1))
    col_local = set_ends(jax.random.randint(part_keys[5], (BLOCKS,), 0, C_DEV), jax.random.fold_in(part_keys[5], 1), 0, C_DEV - 1).astype(jnp.int32)
    row_owner_keys = jax.random.split(jax.random.fold_in(part_keys[6], 1), BLOCKS // BLK_DEV)
    row_owner_turns = jax.random.permutation(jax.random.fold_in(part_keys[6], 3), BLOCKS // BLK_DEV)
    row_owner = jax.vmap(lambda own, number: assign_block(jax.random.fold_in(part_keys[6], 2), own, number, BLK_DEV, N_ROWS, 1, CAP, 1))(row_owner_keys, row_owner_turns).reshape((BLOCKS, 1))
    row_local = set_ends(jax.random.randint(part_keys[7], (BLOCKS,), 0, C_DEV), jax.random.fold_in(part_keys[7], 1), 0, C_DEV - 1).astype(jnp.int32)
    far_rank = set_ends(jax.random.randint(part_keys[8], (FAR_TOT,), RMAX // 8, RMAX + 1), jax.random.fold_in(part_keys[8], 1), RMAX // 8, RMAX).astype(jnp.int32)
    return dict(potential=potential, near_tiles=near_tiles, far_left=far_left, far_right=far_right, col_owner=col_owner, col_local=col_local, row_owner=row_owner, row_local=row_local, far_rank=far_rank)


EPSILON = 1e-06

def apply_matrix(rounded, near_tiles, far_left, far_right, col_global, row_global, far_rank):
    picked = rounded[col_global].reshape(N_ROWS, BLK_DEV, LEAF)
    near_input = picked[:, :NEAR_DEV]
    far_input = picked[:, NEAR_DEV:]

    def near_apply(pair):
        tiles_here, inputs_here = pair
        return jnp.einsum('kij,kj->ki', tiles_here.astype(jnp.float32), inputs_here.astype(jnp.float32), precision=lax.Precision.HIGHEST)
    near_out = lax.map(near_apply, (near_tiles.reshape(N_ROWS, NEAR_DEV, LEAF, LEAF), near_input))
    levels = jnp.arange(RMAX, dtype=jnp.int32)

    def far_apply(group):
        left_here, right_here, inputs_here, rank_here = group
        weights = jnp.einsum('krj,kj->kr', right_here.astype(jnp.float32), inputs_here.astype(jnp.float32), precision=lax.Precision.HIGHEST)
        weights = jnp.where(levels[None, :] < rank_here[:, None], weights, 0.0)
        weights = lax.optimization_barrier(weights.astype(jnp.bfloat16))
        return jnp.einsum('krj,kr->kj', left_here.astype(jnp.float32), weights.astype(jnp.float32), precision=lax.Precision.HIGHEST)
    far_out = lax.map(far_apply, (far_left.reshape(N_ROWS, FAR_DEV, RMAX, LEAF), far_right.reshape(N_ROWS, FAR_DEV, RMAX, LEAF), far_input, far_rank.reshape(N_ROWS, FAR_DEV)))
    block_out = jnp.concatenate([near_out, far_out], axis=1).reshape(BLOCKS, LEAF)
    return jax.ops.segment_sum(block_out, row_global, num_segments=NCL)

def inner(left_field, right_field):
    return jnp.sum(left_field * right_field) / PANELS

def reference(potential, near_tiles, far_left, far_right, col_owner, col_local, row_owner, row_local, far_rank):
    col_global = (col_owner[:, 0] * C_DEV + col_local).astype(jnp.int32)
    row_global = (row_owner[:, 0] * C_DEV + row_local).astype(jnp.int32)

    def product(vector):
        rounded = lax.optimization_barrier(vector.astype(jnp.bfloat16))
        return apply_matrix(rounded, near_tiles, far_left, far_right, col_global, row_global, far_rank)
    beta = jnp.sqrt(inner(potential, potential) + EPSILON)
    first_basis = potential / beta
    image = product(first_basis)
    coef_one = inner(image, first_basis)
    image = image - coef_one * first_basis
    height_one = jnp.sqrt(inner(image, image) + EPSILON)
    second_basis = image / height_one
    image = product(second_basis)
    coef_two = inner(image, first_basis)
    coef_three = inner(image, second_basis)
    image = image - coef_two * first_basis
    image = image - coef_three * second_basis
    height_two = jnp.sqrt(inner(image, image) + EPSILON)
    third_basis = image / height_two
    krylov = jnp.stack([second_basis, third_basis])
    hessen = jnp.stack([beta, coef_one, height_one, coef_two, coef_three, height_two])[None, :]
    return (krylov, hessen)
```

```python
import functools

import jax
import jax.numpy as jnp
from jax import lax
from jax.experimental import pallas as pl
from jax.experimental.pallas import tpu as pltpu
from jax.sharding import PartitionSpec as P

EPSILON = 1e-06
MESH = pl.DeviceIdType.MESH


def total(values):
    return jnp.sum(jnp.sum(values, axis=0, keepdims=True), axis=1, keepdims=True)


def kernel(
    n, potential, near_hbm, left_hbm, right_hbm, col_owner, col_local, row_owner, row_local, far_rank,
    krylov, hessen,
    near, left, right, masks, rank_masks, field_one, field_two, whole_p, whole_i, parts_one, parts_two,
    mine, sums, load_sem, send_sem, recv_sem,
):
    me = lax.axis_index("rows")
    clusters, leaf = potential.shape
    blocks = col_owner.shape[0]
    near_count, far_count, rank = near.shape[0], left.shape[0], left.shape[1]
    rows = n * clusters
    panels = rows * leaf
    f32, bf16 = jnp.float32, jnp.bfloat16

    loads = [
        pltpu.make_async_copy(source, target, load_sem.at[position])
        for position, (source, target) in enumerate(
            [(right_hbm, right), (left_hbm, left), (near_hbm, near)]
        )
    ]
    for load in loads:
        load.start()

    barrier = pltpu.get_barrier_semaphore()

    def greet(step, carry):
        pl.semaphore_signal(
            barrier, inc=1, device_id={"rows": lax.rem(me + step, n)}, device_id_type=MESH
        )
        return carry

    lax.fori_loop(1, n, greet, 0, unroll=n <= 16)
    pl.semaphore_wait(barrier, n - 1)

    def send(phase, source, target):
        def one(step, carry):
            peer = lax.rem(me + step, n)
            pltpu.make_async_remote_copy(
                src_ref=source(peer),
                dst_ref=target.at[me],
                send_sem=send_sem.at[phase],
                recv_sem=recv_sem.at[phase],
                device_id={"rows": peer},
                device_id_type=MESH,
            ).start()
            return carry

        lax.fori_loop(1, n, one, 0, unroll=n <= 16)

    def arrived(phase, target):
        others = target.at[pl.ds(0, n - 1)]
        pltpu.make_async_copy(others, others, recv_sem.at[phase]).wait()

    def sent(phase, target):
        others = target.at[pl.ds(0, n - 1)]
        pltpu.make_async_copy(others, others, send_sem.at[phase]).wait()

    send(0, lambda peer: potential, whole_p)
    whole_p[me] = potential[...]

    def iota(shape, axis):
        return lax.broadcasted_iota(jnp.int32, shape, axis)

    eye = iota((blocks, blocks), 0) == iota((blocks, blocks), 1)
    col_place = jnp.sum(jnp.where(eye, col_local[...].astype(f32), 0.0), axis=1, keepdims=True)
    col_global = col_owner[...].astype(f32) * clusters + col_place
    pick = (iota((blocks, rows), 1).astype(f32) == col_global).astype(f32).astype(bf16)
    row_place = jnp.sum(jnp.where(eye, row_owner[...].astype(f32), 0.0), axis=0, keepdims=True)
    row_global = row_place * clusters + row_local[...].astype(f32)
    place = (iota((rows, blocks), 0).astype(f32) == row_global).astype(f32).astype(bf16)
    for start in range(0, masks.shape[1], leaf):
        lane = start + iota((blocks, leaf), 1)
        if start < near_count * leaf:
            owner = lane // leaf
        else:
            owner = near_count + (lane - near_count * leaf) // rank
        spread = (owner == iota((blocks, leaf), 0)).astype(f32).astype(bf16)
        masks[:, start : start + leaf] = jnp.dot(
            place, spread, preferred_element_type=f32
        ).astype(bf16)
    shape = (far_count, far_count)
    ranks = jnp.sum(
        jnp.where(iota(shape, 0) == iota(shape, 1), far_rank[...].astype(f32), 0.0),
        axis=1, keepdims=True,
    )
    for base in range(0, far_count, 16):
        lane = iota((16, 16 * rank), 1)
        inside = (lane // rank == iota((16, 16 * rank), 0)) & (
            (lane % rank).astype(f32) < ranks[base : base + 16]
        )
        rank_masks[base : base + 16] = inside.astype(f32)

    def wide(row):
        return jnp.broadcast_to(row, (16, row.shape[1])).astype(bf16)

    def spread_out(start, row):
        width = row.shape[1]
        mask = masks[:, start : start + width].reshape(rows // 16, 16, width)
        return (mask * wide(row)[None]).reshape(rows, width)

    def product(vector, field, first_time):
        picked = jnp.dot(pick, vector.astype(bf16), preferred_element_type=f32)
        if first_time:
            loads[0].wait()
        weights = []
        for base in range(0, far_count, 16):
            part = picked[near_count + base : near_count + base + 16].astype(bf16)
            levels = lax.dot_general(
                part, right[base : base + 16].reshape(16 * rank, leaf),
                (((1,), (1,)), ((), ())), preferred_element_type=f32,
            )
            weights.append(
                jnp.sum(levels * rank_masks[base : base + 16], axis=0, keepdims=True)
            )
        if first_time:
            loads[1].wait()
            loads[2].wait()
        result = jnp.zeros((rows, leaf), f32)
        for block in range(near_count):
            result += lax.dot_general(
                spread_out(block * leaf, picked[block : block + 1]), near[block],
                (((1,), (1,)), ((), ())), preferred_element_type=f32,
            )
        for base in range(0, far_count, 16):
            result += jnp.dot(
                spread_out(near_count * leaf + base * rank, weights[base // 16]),
                left[base : base + 16].reshape(16 * rank, leaf),
                preferred_element_type=f32,
            )
        field[...] = result.reshape(n, clusters, leaf)

    def reduce(phase, field, parts):
        send(phase, lambda peer: field.at[peer], parts)
        parts[me] = field[me]

    arrived(0, whole_p)
    pot = whole_p[...].reshape(rows, leaf)
    beta = jnp.sqrt(total(pot * pot) / panels + EPSILON)
    first = pot / beta
    product(first, field_one, True)
    reduce(1, field_one, parts_one)
    arrived(1, parts_one)
    mine[...] = jnp.sum(parts_one[...], axis=0)
    send(2, lambda peer: mine, whole_i)
    whole_i[me] = mine[...]
    first = whole_p[...].reshape(rows, leaf) / beta
    arrived(2, whole_i)
    image = whole_i[...].reshape(rows, leaf)
    h11 = total(image * first) / panels
    image = image - h11 * first
    h21 = jnp.sqrt(total(image * image) / panels + EPSILON)
    second = image / h21
    product(second, field_two, False)
    reduce(3, field_two, parts_two)
    g11 = total(first * first) / panels
    g12 = total(first * second) / panels
    g22 = total(second * second) / panels
    own_first = whole_p[me] / beta
    own_second = (whole_i[me] - h11 * own_first) / h21
    arrived(3, parts_two)
    own = jnp.sum(parts_two[...], axis=0)

    def fold(values):
        values = jnp.sum(values, axis=0, keepdims=True)
        return sum(values[:, at : at + 128] for at in range(0, leaf, 128))

    sums[me, 0:1] = fold(own * own_first)
    sums[me, 1:2] = fold(own * own_second)
    sums[me, 2:3] = fold(own * own)
    sums[me, 3:4] = jnp.zeros((1, 128), f32)
    send(4, lambda peer: sums.at[me], sums)
    arrived(4, sums)
    moments = jnp.sum(jnp.sum(sums[...], axis=0), axis=1, keepdims=True) / panels
    h12, h22, squared = moments[0:1], moments[1:2], moments[2:3]
    squared = (
        squared - 2.0 * (h12 * h12 + h22 * h22)
        + h12 * h12 * g11 + 2.0 * h12 * h22 * g12 + h22 * h22 * g22
    )
    h32 = jnp.sqrt(jnp.maximum(squared, 0.0) + EPSILON)
    krylov[0] = own_second
    krylov[1] = (own - h12 * own_first - h22 * own_second) / h32
    lane = iota(hessen.shape, 1)
    line = jnp.zeros(hessen.shape, f32)
    for position, value in enumerate([beta, h11, h21, h12, h22, h32]):
        line = jnp.where(lane == position, value, line)
    hessen[...] = line
    for phase, target in enumerate([whole_p, parts_one, whole_i, parts_two, sums]):
        sent(phase, target)


def on_device(
    potential, near_tiles, far_left, far_right, col_owner, col_local, row_owner, row_local, far_rank
):
    n = lax.axis_size("rows")
    clusters, leaf = potential.shape
    blocks = col_owner.shape[0]
    near_count = near_tiles.shape[0]
    far_count, rank = far_left.shape[:2]
    rows = n * clusters
    f32, bf16 = jnp.float32, jnp.bfloat16
    vmem = pl.BlockSpec(memory_space=pltpu.VMEM)
    anywhere = pl.BlockSpec(memory_space=pl.ANY)
    slabs = pltpu.VMEM((n, clusters, leaf), f32)
    krylov, hessen = pl.pallas_call(
        functools.partial(kernel, n),
        out_shape=(
            jax.ShapeDtypeStruct((2, clusters, leaf), f32),
            jax.ShapeDtypeStruct((1, 6), f32),
        ),
        in_specs=[vmem, anywhere, anywhere, anywhere] + [vmem] * 5,
        out_specs=(vmem, vmem),
        scratch_shapes=[
            pltpu.VMEM(near_tiles.shape, bf16),
            pltpu.VMEM(far_left.shape, bf16),
            pltpu.VMEM(far_right.shape, bf16),
            pltpu.VMEM((rows, near_count * leaf + far_count * rank), bf16),
            pltpu.VMEM((far_count, 16 * rank), f32),
            slabs, slabs, slabs, slabs, slabs, slabs,
            pltpu.VMEM((clusters, leaf), f32),
            pltpu.VMEM((n, 4, 128), f32),
            pltpu.SemaphoreType.DMA((3,)),
            pltpu.SemaphoreType.DMA((5,)),
            pltpu.SemaphoreType.DMA((5,)),
        ],
        compiler_params=pltpu.CompilerParams(
            collective_id=0, has_side_effects=True, vmem_limit_bytes=56 * 1024 * 1024
        ),
        name="arnoldi",
    )(
        potential, near_tiles, far_left, far_right,
        col_owner, col_local.reshape(1, blocks), row_owner, row_local.reshape(1, blocks),
        far_rank.reshape(1, far_count),
    )
    return (krylov, hessen)


def solution(mesh):
    placed = (
        P(("groups", "rows"), None),
        P(("groups", "rows"), None, None),
        P(("groups", "rows"), None, None),
        P(("groups", "rows"), None, None),
        P(("groups", "rows"), None),
        P(("groups", "rows")),
        P(("groups", "rows"), None),
        P(("groups", "rows")),
        P(("groups", "rows")),
    )
    return jax.shard_map(
        on_device,
        mesh=mesh,
        in_specs=placed,
        out_specs=(P(None, ("groups", "rows"), None), P("groups", None)),
        check_vma=False,
    )
```

```python
import functools

import jax
import jax.numpy as jnp
from jax import lax
from jax.experimental import pallas as pl
from jax.experimental.pallas import tpu as pltpu
from jax.sharding import PartitionSpec as P

EPSILON = 1e-06
MESH = pl.DeviceIdType.MESH


def total(values):
    return jnp.sum(jnp.sum(values, axis=0, keepdims=True), axis=1, keepdims=True)


def kernel(
    n, potential, near_hbm, left_hbm, right_hbm, col_owner, col_local, row_owner, row_local, far_rank,
    krylov, hessen,
    near, left, right, rank_masks, field_one, field_two, whole_p, whole_i, parts_one, parts_two,
    mine, sums, load_sem, send_sem, recv_sem,
):
    me = lax.axis_index("rows")
    clusters, leaf = potential.shape
    blocks = col_owner.shape[1]
    near_count, far_count, rank = near.shape[0], left.shape[0], left.shape[1]
    rows = n * clusters
    panels = rows * leaf
    f32, bf16 = jnp.float32, jnp.bfloat16

    loads = [
        pltpu.make_async_copy(source, target, load_sem.at[position])
        for position, (source, target) in enumerate(
            [(right_hbm, right), (left_hbm, left), (near_hbm, near)]
        )
    ]
    for load in loads:
        load.start()

    barrier = pltpu.get_barrier_semaphore()

    def greet(step, carry):
        pl.semaphore_signal(
            barrier, inc=1, device_id={"rows": lax.rem(me + step, n)}, device_id_type=MESH
        )
        return carry

    lax.fori_loop(1, n, greet, 0, unroll=n <= 16)
    pl.semaphore_wait(barrier, n - 1)

    group, groups = me // 4, n // 4
    upper = group // (groups // 2)
    turned = group + upper * (groups - 1 - 2 * group)

    def peer_at(step):
        place = groups - 1 - step // 4
        place = place - (step // 4 + turned) // (groups - 1)
        place = place + upper * (groups - 1 - 2 * place)
        last = step // (n - 4)
        place = place + last * (group - place)
        return place * 4 + lax.rem(me + 1 + lax.rem(step, 4), 4)

    def send(phase, source, target):
        def one(step, carry):
            peer = peer_at(step)
            pltpu.make_async_remote_copy(
                src_ref=source(peer),
                dst_ref=target.at[me],
                send_sem=send_sem.at[phase],
                recv_sem=recv_sem.at[phase],
                device_id={"rows": peer},
                device_id_type=MESH,
            ).start()
            return carry

        lax.fori_loop(0, n - 1, one, 0, unroll=n <= 16)

    def arrived(phase, target):
        others = target.at[pl.ds(0, n - 1)]
        pltpu.make_async_copy(others, others, recv_sem.at[phase]).wait()

    def sent(phase, target):
        others = target.at[pl.ds(0, n - 1)]
        pltpu.make_async_copy(others, others, send_sem.at[phase]).wait()

    send(0, lambda peer: potential, whole_p)
    whole_p[me] = potential[...]

    def iota(shape, axis):
        return lax.broadcasted_iota(jnp.int32, shape, axis)

    eye = iota((blocks, blocks), 0) == iota((blocks, blocks), 1)
    col_row = (col_owner[...] * clusters + col_local[...]).astype(f32)
    col_global = jnp.sum(jnp.where(eye, col_row, 0.0), axis=1, keepdims=True)
    pick = (iota((blocks, rows), 1).astype(f32) == col_global).astype(f32).astype(bf16)
    row_global = (row_owner[...] * clusters + row_local[...]).astype(f32)
    place = (iota((rows, blocks), 0).astype(f32) == row_global).astype(f32).astype(bf16)
    shape = (far_count, far_count)
    ranks = jnp.sum(
        jnp.where(iota(shape, 0) == iota(shape, 1), far_rank[...].astype(f32), 0.0),
        axis=1, keepdims=True,
    )
    for base in range(0, far_count, 16):
        lane = iota((16, 16 * rank), 1)
        inside = (lane // rank == iota((16, 16 * rank), 0)) & (
            (lane % rank).astype(f32) < ranks[base : base + 16]
        )
        rank_masks[base : base + 16] = inside.astype(f32)

    side = (((1,), (1,)), ((), ()))

    def product(vector, field, first_time):
        picked = jnp.dot(pick, vector.astype(bf16), preferred_element_type=f32).astype(bf16)
        if first_time:
            loads[0].wait()
        weights = []
        for base in range(0, far_count, 16):
            part = picked[near_count + base : near_count + base + 16]
            levels = lax.dot_general(
                part, right[base : base + 16].reshape(16 * rank, leaf), side,
                preferred_element_type=f32,
            )
            weights.append((levels * rank_masks[base : base + 16]).astype(bf16))
        if first_time:
            loads[2].wait()
        results = []
        for base in range(0, near_count, 16):
            part = picked[base : base + 16]
            chosen = jnp.zeros((16, leaf), f32)
            for block in range(16):
                applied = lax.dot_general(
                    part, near[base + block], side, preferred_element_type=f32
                )
                chosen = jnp.where(iota((16, leaf), 0) == block, applied, chosen)
            results.append(chosen)
        if first_time:
            loads[1].wait()
        for base in range(0, far_count, 16):
            results.append(
                jnp.dot(
                    weights[base // 16], left[base : base + 16].reshape(16 * rank, leaf),
                    preferred_element_type=f32,
                )
            )
        rest = jnp.concatenate(results, axis=0)
        result = jnp.zeros((rows, leaf), f32)
        for _ in range(3):
            term = rest.astype(bf16)
            rest = rest - term.astype(f32)
            result += jnp.dot(place, term, preferred_element_type=f32)
        field[...] = result.reshape(n, clusters, leaf)

    def reduce(phase, field, parts):
        send(phase, lambda peer: field.at[peer], parts)
        parts[me] = field[me]

    arrived(0, whole_p)
    pot = whole_p[...].reshape(rows, leaf)
    beta = jnp.sqrt(total(pot * pot) / panels + EPSILON)
    first = pot / beta
    product(first, field_one, True)
    reduce(1, field_one, parts_one)
    arrived(1, parts_one)
    mine[...] = jnp.sum(parts_one[...], axis=0)
    send(2, lambda peer: mine, whole_i)
    whole_i[me] = mine[...]
    first = whole_p[...].reshape(rows, leaf) / beta
    arrived(2, whole_i)
    image = whole_i[...].reshape(rows, leaf)
    h11 = total(image * first) / panels
    image = image - h11 * first
    h21 = jnp.sqrt(total(image * image) / panels + EPSILON)
    second = image / h21
    product(second, field_two, False)
    reduce(3, field_two, parts_two)
    g11 = total(first * first) / panels
    g12 = total(first * second) / panels
    g22 = total(second * second) / panels
    own_first = whole_p[me] / beta
    own_second = (whole_i[me] - h11 * own_first) / h21
    arrived(3, parts_two)
    own = jnp.sum(parts_two[...], axis=0)

    def fold(values):
        values = jnp.sum(values, axis=0, keepdims=True)
        return sum(values[:, at : at + 128] for at in range(0, leaf, 128))

    sums[me, 0:1] = fold(own * own_first)
    sums[me, 1:2] = fold(own * own_second)
    sums[me, 2:3] = fold(own * own)
    sums[me, 3:4] = jnp.zeros((1, 128), f32)
    send(4, lambda peer: sums.at[me], sums)
    arrived(4, sums)
    moments = jnp.sum(jnp.sum(sums[...], axis=0), axis=1, keepdims=True) / panels
    h12, h22, squared = moments[0:1], moments[1:2], moments[2:3]
    squared = (
        squared - 2.0 * (h12 * h12 + h22 * h22)
        + h12 * h12 * g11 + 2.0 * h12 * h22 * g12 + h22 * h22 * g22
    )
    h32 = jnp.sqrt(jnp.maximum(squared, 0.0) + EPSILON)
    krylov[0] = own_second
    krylov[1] = (own - h12 * own_first - h22 * own_second) / h32
    lane = iota(hessen.shape, 1)
    line = jnp.zeros(hessen.shape, f32)
    for position, value in enumerate([beta, h11, h21, h12, h22, h32]):
        line = jnp.where(lane == position, value, line)
    hessen[...] = line
    for phase, target in enumerate([whole_p, parts_one, whole_i, parts_two, sums]):
        sent(phase, target)


def hand_over(krylov_in, hessen_in, krylov, hessen):
    krylov[...] = krylov_in[...]
    hessen[...] = hessen_in[...]


def on_device(
    potential, near_tiles, far_left, far_right, col_owner, col_local, row_owner, row_local, far_rank
):
    n = lax.axis_size("rows")
    clusters, leaf = potential.shape
    blocks = col_owner.shape[0]
    near_count = near_tiles.shape[0]
    far_count, rank = far_left.shape[:2]
    rows = n * clusters
    f32, bf16 = jnp.float32, jnp.bfloat16
    vmem = pl.BlockSpec(memory_space=pltpu.VMEM)
    anywhere = pl.BlockSpec(memory_space=pl.ANY)
    slabs = pltpu.VMEM((n, clusters, leaf), f32)
    krylov, hessen = pl.pallas_call(
        functools.partial(kernel, n),
        out_shape=(
            jax.ShapeDtypeStruct((2, clusters, leaf), f32),
            jax.ShapeDtypeStruct((1, 6), f32),
        ),
        in_specs=[vmem, anywhere, anywhere, anywhere] + [vmem] * 5,
        out_specs=(vmem, vmem),
        scratch_shapes=[
            pltpu.VMEM(near_tiles.shape, bf16),
            pltpu.VMEM(far_left.shape, bf16),
            pltpu.VMEM(far_right.shape, bf16),
            pltpu.VMEM((far_count, 16 * rank), f32),
            slabs, slabs, slabs, slabs, slabs, slabs,
            pltpu.VMEM((clusters, leaf), f32),
            pltpu.VMEM((n, 4, 128), f32),
            pltpu.SemaphoreType.DMA((3,)),
            pltpu.SemaphoreType.DMA((5,)),
            pltpu.SemaphoreType.DMA((5,)),
        ],
        compiler_params=pltpu.CompilerParams(
            collective_id=0, has_side_effects=True, vmem_limit_bytes=56 * 1024 * 1024
        ),
        name="arnoldi",
    )(
        potential, near_tiles, far_left, far_right,
        col_owner.reshape(1, blocks), col_local.reshape(1, blocks),
        row_owner.reshape(1, blocks), row_local.reshape(1, blocks),
        far_rank.reshape(1, far_count),
    )
    return pl.pallas_call(
        hand_over,
        out_shape=(
            jax.ShapeDtypeStruct((2, clusters, leaf), f32),
            jax.ShapeDtypeStruct((1, 6), f32),
        ),
        in_specs=[vmem, vmem],
        out_specs=(vmem, vmem),
        name="hand_over",
    )(krylov, hessen)


def solution(mesh):
    placed = (
        P(("groups", "rows"), None),
        P(("groups", "rows"), None, None),
        P(("groups", "rows"), None, None),
        P(("groups", "rows"), None, None),
        P(("groups", "rows"), None),
        P(("groups", "rows")),
        P(("groups", "rows"), None),
        P(("groups", "rows")),
        P(("groups", "rows")),
    )
    return jax.shard_map(
        on_device,
        mesh=mesh,
        in_specs=placed,
        out_specs=(P(None, ("groups", "rows"), None), P("groups", None)),
        check_vma=False,
    )
```

```python
import functools

import jax
import jax.numpy as jnp
from jax import lax
from jax.experimental import pallas as pl
from jax.experimental.pallas import tpu as pltpu
from jax.sharding import PartitionSpec as P

EPSILON = 1e-06
MESH = pl.DeviceIdType.MESH


def total(values):
    return jnp.sum(jnp.sum(values, axis=0, keepdims=True), axis=1, keepdims=True)


def kernel(
    n, potential_in, near_hbm, left_hbm, right_hbm, col_owner_in, col_local_in, row_owner_in,
    row_local_in, far_rank_in,
    krylov, hessen,
    potential, col_owner, col_local, row_owner, row_local, far_rank,
    near, left, right, rank_masks, field_one, field_two, whole_p, whole_i, parts_one, parts_two,
    sums, load_sem, send_sem, recv_sem,
):
    me = lax.axis_index("rows")
    clusters, leaf = potential.shape
    blocks = col_owner.shape[1]
    near_count, far_count, rank = near.shape[0], left.shape[0], left.shape[1]
    rows = n * clusters
    panels = rows * leaf
    f32, bf16 = jnp.float32, jnp.bfloat16

    group, groups = lax.div(me, 4), n // 4
    upper = lax.div(group, groups // 2)
    turned = group + upper * (groups - 1 - 2 * group)

    def peer_at(step):
        place = groups - 1 - step // 4
        place = place - lax.div(step // 4 + turned, groups - 1)
        place = place + upper * (groups - 1 - 2 * place)
        last = step // (n - 4)
        place = place + last * (group - place)
        return place * 4 + lax.rem(me + 1 + step % 4, 4)

    peers = [peer_at(step) for step in range(n - 1)]

    barrier = pltpu.get_barrier_semaphore()
    for peer in peers:
        pl.semaphore_signal(barrier, inc=1, device_id={"rows": peer}, device_id_type=MESH)

    loads = [
        pltpu.make_async_copy(source, target, load_sem.at[position])
        for position, (source, target) in enumerate(
            [
                (right_hbm, right), (left_hbm, left), (near_hbm, near), (potential_in, potential),
                (col_owner_in, col_owner), (col_local_in, col_local), (row_owner_in, row_owner),
                (row_local_in, row_local), (far_rank_in, far_rank),
            ]
        )
    ]
    for load in loads[3:] + loads[:3]:
        load.start()
    for load in loads[3:]:
        load.wait()
    pl.semaphore_wait(barrier, n - 1)

    def send(phase, source, target):
        for peer in peers:
            pltpu.make_async_remote_copy(
                src_ref=source(peer),
                dst_ref=target.at[me],
                send_sem=send_sem.at[phase],
                recv_sem=recv_sem.at[phase],
                device_id={"rows": peer},
                device_id_type=MESH,
            ).start()

    def arrived(phase, target):
        others = target.at[pl.ds(0, n - 1)]
        pltpu.make_async_copy(others, others, recv_sem.at[phase]).wait()

    def sent(phase, target):
        others = target.at[pl.ds(0, n - 1)]
        pltpu.make_async_copy(others, others, send_sem.at[phase]).wait()

    send(0, lambda peer: potential, whole_p)
    whole_p[me] = potential[...]

    def iota(shape, axis):
        return lax.broadcasted_iota(jnp.int32, shape, axis)

    eye = iota((blocks, blocks), 0) == iota((blocks, blocks), 1)
    col_row = (col_owner[...] * clusters + col_local[...]).astype(f32)
    col_global = jnp.sum(jnp.where(eye, col_row, 0.0), axis=1, keepdims=True)
    pick = (iota((blocks, rows), 1).astype(f32) == col_global).astype(f32).astype(bf16)
    row_global = (row_owner[...] * clusters + row_local[...]).astype(f32)
    row_column = jnp.sum(jnp.where(eye, row_global, 0.0), axis=1, keepdims=True)
    thrice = lax.rem(iota((blocks, 3 * blocks), 1), blocks) == iota((blocks, 3 * blocks), 0)
    row_thrice = jnp.sum(jnp.where(thrice, row_column, 0.0), axis=0, keepdims=True)
    place = (iota((rows, 3 * blocks), 0).astype(f32) == row_thrice).astype(f32).astype(bf16)
    shape = (far_count, far_count)
    ranks = jnp.sum(
        jnp.where(iota(shape, 0) == iota(shape, 1), far_rank[...].astype(f32), 0.0),
        axis=1, keepdims=True,
    )
    for base in range(0, far_count, 16):
        lane = iota((16, 16 * rank), 1)
        inside = (lane // rank == iota((16, 16 * rank), 0)) & (
            (lane % rank).astype(f32) < ranks[base : base + 16]
        )
        rank_masks[base : base + 16] = inside.astype(f32)

    side = (((1,), (1,)), ((), ()))

    def product(vector, field, first_time):
        picked = jnp.dot(pick, vector.astype(bf16), preferred_element_type=f32).astype(bf16)
        if first_time:
            loads[0].wait()
        weights = []
        for base in range(0, far_count, 16):
            part = picked[near_count + base : near_count + base + 16]
            levels = lax.dot_general(
                part, right[base : base + 16].reshape(16 * rank, leaf), side,
                preferred_element_type=f32,
            )
            weights.append((levels * rank_masks[base : base + 16]).astype(bf16))
        if first_time:
            loads[2].wait()
        results = []
        for base in range(0, near_count, 16):
            part = picked[base : base + 16]
            chosen = jnp.zeros((16, leaf), f32)
            for block in range(16):
                applied = lax.dot_general(
                    part, near[base + block], side, preferred_element_type=f32
                )
                chosen = jnp.where(iota((16, leaf), 0) == block, applied, chosen)
            results.append(chosen)
        if first_time:
            loads[1].wait()
        for base in range(0, far_count, 16):
            results.append(
                jnp.dot(
                    weights[base // 16], left[base : base + 16].reshape(16 * rank, leaf),
                    preferred_element_type=f32,
                )
            )
        rest = jnp.concatenate(results, axis=0)
        terms = []
        for _ in range(3):
            terms.append(rest.astype(bf16))
            rest = rest - terms[-1].astype(f32)
        result = jnp.dot(place, jnp.concatenate(terms, axis=0), preferred_element_type=f32)
        field[...] = result.reshape(n, clusters, leaf)

    def reduce(phase, field, parts):
        send(phase, lambda peer: field.at[peer], parts)
        parts[me] = field[me]

    arrived(0, whole_p)
    pot = whole_p[...].reshape(rows, leaf)
    beta = jnp.sqrt(total(pot * pot) / panels + EPSILON)
    first = pot / beta
    product(first, field_one, True)
    reduce(1, field_one, parts_one)
    arrived(1, parts_one)
    mine = jnp.sum(parts_one[...], axis=0)
    middle = leaf // 2
    whole_i[me] = jnp.concatenate([mine[:, :middle], mine[:, middle:]], axis=0).astype(bf16)
    send(2, lambda peer: whole_i.at[me], whole_i)
    first = whole_p[...].reshape(rows, leaf) / beta
    arrived(2, whole_i)
    image = whole_i[...].astype(f32)
    image = jnp.concatenate(
        [image[:, :clusters].reshape(rows, middle), image[:, clusters:].reshape(rows, middle)], axis=1
    )
    h11 = total(image * first) / panels
    image = image - h11 * first
    h21 = jnp.sqrt(total(image * image) / panels + EPSILON)
    second = image / h21
    product(second, field_two, False)
    reduce(3, field_two, parts_two)
    g11 = total(first * first) / panels
    g12 = total(first * second) / panels
    g22 = total(second * second) / panels
    own_first = whole_p[me] / beta
    own_second = (mine - h11 * own_first) / h21
    arrived(3, parts_two)
    own = jnp.sum(parts_two[...], axis=0)

    def fold(values):
        values = jnp.sum(values, axis=0, keepdims=True)
        return sum(values[:, at : at + 128] for at in range(0, leaf, 128))

    sums[me, 0:1] = fold(own * own_first)
    sums[me, 1:2] = fold(own * own_second)
    sums[me, 2:3] = fold(own * own)
    sums[me, 3:4] = jnp.zeros((1, 128), f32)
    send(4, lambda peer: sums.at[me], sums)
    arrived(4, sums)
    moments = jnp.sum(jnp.sum(sums[...], axis=0), axis=1, keepdims=True) / panels
    h12, h22, squared = moments[0:1], moments[1:2], moments[2:3]
    squared = (
        squared - 2.0 * (h12 * h12 + h22 * h22)
        + h12 * h12 * g11 + 2.0 * h12 * h22 * g12 + h22 * h22 * g22
    )
    h32 = jnp.sqrt(jnp.maximum(squared, 0.0) + EPSILON)
    krylov[0] = own_second
    krylov[1] = (own - h12 * own_first - h22 * own_second) / h32
    lane = iota(hessen.shape, 1)
    line = jnp.zeros(hessen.shape, f32)
    for position, value in enumerate([beta, h11, h21, h12, h22, h32]):
        line = jnp.where(lane == position, value, line)
    hessen[...] = line
    for phase, target in enumerate([whole_p, parts_one, whole_i, parts_two, sums]):
        sent(phase, target)


def on_device(
    potential, near_tiles, far_left, far_right, col_owner, col_local, row_owner, row_local, far_rank
):
    n = lax.axis_size("rows")
    clusters, leaf = potential.shape
    blocks = col_owner.shape[0]
    near_count = near_tiles.shape[0]
    far_count, rank = far_left.shape[:2]
    rows = n * clusters
    f32, bf16 = jnp.float32, jnp.bfloat16
    vmem = pl.BlockSpec(memory_space=pltpu.VMEM)
    anywhere = pl.BlockSpec(memory_space=pl.ANY)
    slabs = pltpu.VMEM((n, clusters, leaf), f32)
    krylov, hessen = pl.pallas_call(
        functools.partial(kernel, n),
        out_shape=(pltpu.VMEM((2, clusters, leaf), f32), pltpu.VMEM((1, 6), f32)),
        in_specs=[anywhere] * 9,
        out_specs=(vmem, vmem),
        scratch_shapes=[
            pltpu.VMEM((clusters, leaf), f32),
            pltpu.VMEM((1, blocks), jnp.int32),
            pltpu.VMEM((1, blocks), jnp.int32),
            pltpu.VMEM((1, blocks), jnp.int32),
            pltpu.VMEM((1, blocks), jnp.int32),
            pltpu.VMEM((1, far_count), jnp.int32),
            pltpu.VMEM(near_tiles.shape, bf16),
            pltpu.VMEM(far_left.shape, bf16),
            pltpu.VMEM(far_right.shape, bf16),
            pltpu.VMEM((far_count, 16 * rank), f32),
            slabs, slabs, slabs,
            pltpu.VMEM((n, 2 * clusters, leaf // 2), bf16),
            slabs, slabs,
            pltpu.VMEM((n, 4, 128), f32),
            pltpu.SemaphoreType.DMA((9,)),
            pltpu.SemaphoreType.DMA((5,)),
            pltpu.SemaphoreType.DMA((5,)),
        ],
        compiler_params=pltpu.CompilerParams(
            collective_id=0, has_side_effects=True, vmem_limit_bytes=56 * 1024 * 1024
        ),
        name="arnoldi",
    )(
        potential, near_tiles, far_left, far_right,
        col_owner.reshape(1, blocks), col_local.reshape(1, blocks),
        row_owner.reshape(1, blocks), row_local.reshape(1, blocks),
        far_rank.reshape(1, far_count),
    )
    return (krylov, hessen)


def solution(mesh):
    placed = (
        P(("groups", "rows"), None),
        P(("groups", "rows"), None, None),
        P(("groups", "rows"), None, None),
        P(("groups", "rows"), None, None),
        P(("groups", "rows"), None),
        P(("groups", "rows")),
        P(("groups", "rows"), None),
        P(("groups", "rows")),
        P(("groups", "rows")),
    )
    return jax.shard_map(
        on_device,
        mesh=mesh,
        in_specs=placed,
        out_specs=(P(None, ("groups", "rows"), None), P("groups", None)),
        check_vma=False,
    )
```

```python
import functools

import jax
import jax.numpy as jnp
from jax import lax
from jax.experimental import pallas as pl
from jax.experimental.pallas import tpu as pltpu
from jax.sharding import PartitionSpec as P

EPSILON = 1e-06
MESH = pl.DeviceIdType.MESH


def total(values):
    return jnp.sum(jnp.sum(values, axis=0, keepdims=True), axis=1, keepdims=True)


def kernel(
    n, potential_in, near_hbm, left_hbm, right_hbm, col_owner_in, col_local_in, row_owner_in,
    row_local_in, far_rank_in,
    krylov, hessen,
    potential, col_owner, col_local, row_owner, row_local, far_rank,
    near, left, right, turned_right, rank_masks, field_one, field_two, whole_p, whole_i, parts_one, parts_two,
    sums, load_sem, send_sem, recv_sem,
):
    me = lax.axis_index("rows")
    clusters, leaf = potential.shape
    blocks = col_owner.shape[1]
    near_count, far_count, rank = near.shape[0], left.shape[0], left.shape[1]
    rows = n * clusters
    panels = rows * leaf
    f32, bf16 = jnp.float32, jnp.bfloat16

    group, groups = lax.div(me, 4), n // 4
    upper = lax.div(group, groups // 2)
    turned = group + upper * (groups - 1 - 2 * group)

    def peer_at(step):
        place = groups - 1 - step // 4
        place = place - lax.div(step // 4 + turned, groups - 1)
        place = place + upper * (groups - 1 - 2 * place)
        last = step // (n - 4)
        place = place + last * (group - place)
        return place * 4 + lax.rem(me + 1 + step % 4, 4)

    peers = [peer_at(step) for step in range(n - 1)]

    barrier = pltpu.get_barrier_semaphore()
    for peer in peers:
        pl.semaphore_signal(barrier, inc=1, device_id={"rows": peer}, device_id_type=MESH)

    loads = [
        pltpu.make_async_copy(source, target, load_sem.at[position])
        for position, (source, target) in enumerate(
            [
                (right_hbm, right), (left_hbm, left), (near_hbm, near), (potential_in, potential),
                (col_owner_in, col_owner), (col_local_in, col_local), (row_owner_in, row_owner),
                (row_local_in, row_local), (far_rank_in, far_rank),
            ]
        )
    ]
    for load in loads[3:] + loads[:3]:
        load.start()
    for load in loads[3:]:
        load.wait()
    pl.semaphore_wait(barrier, n - 1)

    def send(phase, source, target):
        for peer in peers:
            pltpu.make_async_remote_copy(
                src_ref=source(peer),
                dst_ref=target.at[me],
                send_sem=send_sem.at[phase],
                recv_sem=recv_sem.at[phase],
                device_id={"rows": peer},
                device_id_type=MESH,
            ).start()

    def arrived(phase, target):
        others = target.at[pl.ds(0, n - 1)]
        pltpu.make_async_copy(others, others, recv_sem.at[phase]).wait()

    def sent(phase, target):
        others = target.at[pl.ds(0, n - 1)]
        pltpu.make_async_copy(others, others, send_sem.at[phase]).wait()

    send(0, lambda peer: potential, whole_p)
    whole_p[me] = potential[...]

    def iota(shape, axis):
        return lax.broadcasted_iota(jnp.int32, shape, axis)

    eye = iota((blocks, blocks), 0) == iota((blocks, blocks), 1)
    col_row = (col_owner[...] * clusters + col_local[...]).astype(f32)
    col_global = jnp.sum(jnp.where(eye, col_row, 0.0), axis=1, keepdims=True)
    pick = (iota((blocks, rows), 1).astype(f32) == col_global).astype(f32).astype(bf16)
    row_global = (row_owner[...] * clusters + row_local[...]).astype(f32)
    row_column = jnp.sum(jnp.where(eye, row_global, 0.0), axis=1, keepdims=True)
    thrice = lax.rem(iota((blocks, 3 * blocks), 1), blocks) == iota((blocks, 3 * blocks), 0)
    row_thrice = jnp.sum(jnp.where(thrice, row_column, 0.0), axis=0, keepdims=True)
    place = (iota((rows, 3 * blocks), 0).astype(f32) == row_thrice).astype(f32).astype(bf16)
    shape = (far_count, far_count)
    ranks = jnp.sum(
        jnp.where(iota(shape, 0) == iota(shape, 1), far_rank[...].astype(f32), 0.0),
        axis=1, keepdims=True,
    )
    for base in range(0, far_count, 16):
        lane = iota((16, 16 * rank), 1)
        inside = (lane // rank == iota((16, 16 * rank), 0)) & (
            (lane % rank).astype(f32) < ranks[base : base + 16]
        )
        rank_masks[base : base + 16] = inside.astype(f32)

    side = (((1,), (1,)), ((), ()))

    def product(vector, field, first_time):
        picked = jnp.dot(pick, vector.astype(bf16), preferred_element_type=f32).astype(bf16)
        weights = []
        for base in range(0, far_count, 16):
            part = picked[near_count + base : near_count + base + 16]
            levels = jnp.concatenate(
                [
                    jnp.dot(part, turned_right[base // 4 + at], preferred_element_type=f32)
                    for at in range(4)
                ],
                axis=1,
            )
            weights.append((levels * rank_masks[base : base + 16]).astype(bf16))
        results = []
        for base in range(0, near_count, 16):
            part = picked[base : base + 16]
            chosen = jnp.zeros((16, leaf), f32)
            for block in range(16):
                applied = jnp.dot(part, near[base + block], preferred_element_type=f32)
                chosen = jnp.where(iota((16, leaf), 0) == block, applied, chosen)
            results.append(chosen)
        if first_time:
            loads[1].wait()
        for base in range(0, far_count, 16):
            results.append(
                jnp.dot(
                    weights[base // 16], left[base : base + 16].reshape(16 * rank, leaf),
                    preferred_element_type=f32,
                )
            )
        rest = jnp.concatenate(results, axis=0)
        terms = []
        for _ in range(3):
            terms.append(rest.astype(bf16))
            rest = rest - terms[-1].astype(f32)
        result = jnp.dot(place, jnp.concatenate(terms, axis=0), preferred_element_type=f32)
        field[...] = result.reshape(n, clusters, leaf)

    def reduce(phase, field, parts):
        send(phase, lambda peer: field.at[peer], parts)
        parts[me] = field[me]

    loads[2].wait()
    for block in range(near_count):
        near[block] = near[block].T
    loads[0].wait()
    for base in range(0, far_count, 4):
        turned_right[base // 4] = right[base : base + 4].reshape(4 * rank, leaf).T
    arrived(0, whole_p)
    pot = whole_p[...].reshape(rows, leaf)
    beta = jnp.sqrt(total(pot * pot) / panels + EPSILON)
    scale = 1.0 / beta
    product(pot * scale, field_one, True)
    reduce(1, field_one, parts_one)
    first = whole_p[...].reshape(rows, leaf) * scale
    whole_p[...] = first.reshape(n, clusters, leaf)
    g11 = total(first * first) / panels
    arrived(1, parts_one)
    mine = jnp.sum(parts_one[...], axis=0)
    middle = leaf // 2
    whole_i[me] = jnp.concatenate([mine[:, :middle], mine[:, middle:]], axis=0).astype(bf16)
    send(2, lambda peer: whole_i.at[me], whole_i)
    first = whole_p[...].reshape(rows, leaf)
    arrived(2, whole_i)
    image = whole_i[...].astype(f32)
    image = jnp.concatenate(
        [image[:, :clusters].reshape(rows, middle), image[:, clusters:].reshape(rows, middle)], axis=1
    )
    h11 = total(image * first) / panels
    squared = total(image * image) / panels + h11 * h11 * (g11 - 2.0)
    h21 = jnp.sqrt(jnp.maximum(squared, 0.0) + EPSILON)
    scale = 1.0 / h21
    second = (image - h11 * first) * scale
    product(second, field_two, False)
    reduce(3, field_two, parts_two)
    g12 = total(first * second) / panels
    g22 = total(second * second) / panels
    own_first = whole_p[me]
    own_second = (mine - h11 * own_first) * scale
    arrived(3, parts_two)
    own = jnp.sum(parts_two[...], axis=0)

    def fold(values):
        values = jnp.sum(values, axis=0, keepdims=True)
        return sum(values[:, at : at + 128] for at in range(0, leaf, 128))

    sums[me, 0:1] = fold(own * own_first)
    sums[me, 1:2] = fold(own * own_second)
    sums[me, 2:3] = fold(own * own)
    sums[me, 3:4] = jnp.zeros((1, 128), f32)
    send(4, lambda peer: sums.at[me], sums)
    arrived(4, sums)
    moments = jnp.sum(jnp.sum(sums[...], axis=0), axis=1, keepdims=True) / panels
    h12, h22, squared = moments[0:1], moments[1:2], moments[2:3]
    squared = (
        squared - 2.0 * (h12 * h12 + h22 * h22)
        + h12 * h12 * g11 + 2.0 * h12 * h22 * g12 + h22 * h22 * g22
    )
    h32 = jnp.sqrt(jnp.maximum(squared, 0.0) + EPSILON)
    krylov[0] = own_second
    krylov[1] = (own - h12 * own_first - h22 * own_second) / h32
    lane = iota(hessen.shape, 1)
    line = jnp.zeros(hessen.shape, f32)
    for position, value in enumerate([beta, h11, h21, h12, h22, h32]):
        line = jnp.where(lane == position, value, line)
    hessen[...] = line
    for phase, target in enumerate([whole_p, parts_one, whole_i, parts_two, sums]):
        sent(phase, target)


def on_device(
    potential, near_tiles, far_left, far_right, col_owner, col_local, row_owner, row_local, far_rank
):
    n = lax.axis_size("rows")
    clusters, leaf = potential.shape
    blocks = col_owner.shape[0]
    near_count = near_tiles.shape[0]
    far_count, rank = far_left.shape[:2]
    rows = n * clusters
    f32, bf16 = jnp.float32, jnp.bfloat16
    vmem = pl.BlockSpec(memory_space=pltpu.VMEM)
    anywhere = pl.BlockSpec(memory_space=pl.ANY)
    slabs = pltpu.VMEM((n, clusters, leaf), f32)
    krylov, hessen = pl.pallas_call(
        functools.partial(kernel, n),
        out_shape=(pltpu.VMEM((2, clusters, leaf), f32), pltpu.VMEM((1, 6), f32)),
        in_specs=[anywhere] * 9,
        out_specs=(vmem, vmem),
        scratch_shapes=[
            pltpu.VMEM((clusters, leaf), f32),
            pltpu.VMEM((1, blocks), jnp.int32),
            pltpu.VMEM((1, blocks), jnp.int32),
            pltpu.VMEM((1, blocks), jnp.int32),
            pltpu.VMEM((1, blocks), jnp.int32),
            pltpu.VMEM((1, far_count), jnp.int32),
            pltpu.VMEM(near_tiles.shape, bf16),
            pltpu.VMEM(far_left.shape, bf16),
            pltpu.VMEM(far_right.shape, bf16),
            pltpu.VMEM((far_count // 4, leaf, 4 * rank), bf16),
            pltpu.VMEM((far_count, 16 * rank), f32),
            slabs, slabs, slabs,
            pltpu.VMEM((n, 2 * clusters, leaf // 2), bf16),
            slabs, slabs,
            pltpu.VMEM((n, 4, 128), f32),
            pltpu.SemaphoreType.DMA((9,)),
            pltpu.SemaphoreType.DMA((5,)),
            pltpu.SemaphoreType.DMA((5,)),
        ],
        compiler_params=pltpu.CompilerParams(
            collective_id=0, has_side_effects=True, vmem_limit_bytes=56 * 1024 * 1024
        ),
        name="arnoldi",
    )(
        potential, near_tiles, far_left, far_right,
        col_owner.reshape(1, blocks), col_local.reshape(1, blocks),
        row_owner.reshape(1, blocks), row_local.reshape(1, blocks),
        far_rank.reshape(1, far_count),
    )
    return (krylov, hessen)


def solution(mesh):
    placed = (
        P(("groups", "rows"), None),
        P(("groups", "rows"), None, None),
        P(("groups", "rows"), None, None),
        P(("groups", "rows"), None, None),
        P(("groups", "rows"), None),
        P(("groups", "rows")),
        P(("groups", "rows"), None),
        P(("groups", "rows")),
        P(("groups", "rows")),
    )
    return jax.shard_map(
        on_device,
        mesh=mesh,
        in_specs=placed,
        out_specs=(P(None, ("groups", "rows"), None), P("groups", None)),
        check_vma=False,
    )
```

```python
import functools

import jax
import jax.numpy as jnp
from jax import lax
from jax.experimental import pallas as pl
from jax.experimental.pallas import tpu as pltpu
from jax.sharding import PartitionSpec as P

EPSILON = 1e-06
MESH = pl.DeviceIdType.MESH


def total(values):
    return jnp.sum(jnp.sum(values, axis=0, keepdims=True), axis=1, keepdims=True)


def kernel(
    n, potential_in, near_hbm, left_hbm, right_hbm, col_owner_in, col_local_in, row_owner_in,
    row_local_in, far_rank_in,
    krylov, hessen,
    potential, col_owner, col_local, row_owner, row_local, far_rank,
    near, left, right, turned_right, rank_masks, field_one, field_two, whole_p, whole_i, parts_one, parts_two,
    sums, load_sem, send_sem, recv_sem,
):
    me = lax.axis_index("rows")
    clusters, leaf = potential.shape
    blocks = col_owner.shape[1]
    near_count, far_count, rank = near.shape[0], left.shape[0], left.shape[1]
    rows = n * clusters
    panels = rows * leaf
    f32, bf16 = jnp.float32, jnp.bfloat16

    group, groups = lax.div(me, 4), n // 4
    upper = lax.div(group, groups // 2)
    turned = group + upper * (groups - 1 - 2 * group)

    def peer_at(step):
        place = groups - 1 - step // 4
        place = place - lax.div(step // 4 + turned, groups - 1)
        place = place + upper * (groups - 1 - 2 * place)
        last = step // (n - 4)
        place = place + last * (group - place)
        return place * 4 + lax.rem(me + 1 + step % 4, 4)

    peers = [peer_at(step) for step in range(n - 1)]

    barrier = pltpu.get_barrier_semaphore()
    for peer in peers:
        pl.semaphore_signal(barrier, inc=1, device_id={"rows": peer}, device_id_type=MESH)

    loads = [
        pltpu.make_async_copy(source, target, load_sem.at[position])
        for position, (source, target) in enumerate(
            [
                (right_hbm, right), (left_hbm, left), (near_hbm, near), (potential_in, potential),
                (col_owner_in, col_owner), (col_local_in, col_local), (row_owner_in, row_owner),
                (row_local_in, row_local), (far_rank_in, far_rank),
            ]
        )
    ]
    for load in loads[3:] + [loads[0], loads[2], loads[1]]:
        load.start()
    for load in loads[3:]:
        load.wait()
    pl.semaphore_wait(barrier, n - 1)

    def send(phase, source, target):
        for peer in peers:
            pltpu.make_async_remote_copy(
                src_ref=source(peer),
                dst_ref=target.at[me],
                send_sem=send_sem.at[phase],
                recv_sem=recv_sem.at[phase],
                device_id={"rows": peer},
                device_id_type=MESH,
            ).start()

    def arrived(phase, target):
        others = target.at[pl.ds(0, n - 1)]
        pltpu.make_async_copy(others, others, recv_sem.at[phase]).wait()

    def sent(phase, target):
        others = target.at[pl.ds(0, n - 1)]
        pltpu.make_async_copy(others, others, send_sem.at[phase]).wait()

    send(0, lambda peer: potential, whole_p)
    whole_p[me] = potential[...]

    def iota(shape, axis):
        return lax.broadcasted_iota(jnp.int32, shape, axis)

    eye = iota((blocks, blocks), 0) == iota((blocks, blocks), 1)
    col_row = (col_owner[...] * clusters + col_local[...]).astype(f32)
    col_global = jnp.sum(jnp.where(eye, col_row, 0.0), axis=1, keepdims=True)
    pick = (iota((blocks, rows), 1).astype(f32) == col_global).astype(f32).astype(bf16)
    row_global = (row_owner[...] * clusters + row_local[...]).astype(f32)
    row_column = jnp.sum(jnp.where(eye, row_global, 0.0), axis=1, keepdims=True)
    thrice = lax.rem(iota((blocks, 3 * blocks), 1), blocks) == iota((blocks, 3 * blocks), 0)
    row_thrice = jnp.sum(jnp.where(thrice, row_column, 0.0), axis=0, keepdims=True)
    place = (iota((rows, 3 * blocks), 0).astype(f32) == row_thrice).astype(f32).astype(bf16)
    shape = (far_count, far_count)
    ranks = jnp.sum(
        jnp.where(iota(shape, 0) == iota(shape, 1), far_rank[...].astype(f32), 0.0),
        axis=1, keepdims=True,
    )
    for base in range(0, far_count, 16):
        lane = iota((16, 16 * rank), 1)
        inside = (lane // rank == iota((16, 16 * rank), 0)) & (
            (lane % rank).astype(f32) < ranks[base : base + 16]
        )
        rank_masks[base : base + 16] = inside.astype(f32)

    side = (((1,), (1,)), ((), ()))

    def product(vector, field, first_time):
        picked = jnp.dot(pick, vector.astype(bf16), preferred_element_type=f32).astype(bf16)
        weights = []
        for base in range(0, far_count, 16):
            part = picked[near_count + base : near_count + base + 16]
            levels = jnp.concatenate(
                [
                    jnp.dot(part, turned_right[base // 4 + at], preferred_element_type=f32)
                    for at in range(4)
                ],
                axis=1,
            )
            weights.append((levels * rank_masks[base : base + 16]).astype(bf16))
        results = []
        for base in range(0, near_count, 16):
            part = picked[base : base + 16]
            chosen = jnp.zeros((16, leaf), f32)
            for block in range(16):
                applied = jnp.dot(part, near[base + block], preferred_element_type=f32)
                chosen = jnp.where(iota((16, leaf), 0) == block, applied, chosen)
            results.append(chosen)
        if first_time:
            loads[1].wait()
        for base in range(0, far_count, 16):
            results.append(
                jnp.dot(
                    weights[base // 16], left[base : base + 16].reshape(16 * rank, leaf),
                    preferred_element_type=f32,
                )
            )
        rest = jnp.concatenate(results, axis=0)
        terms = []
        for _ in range(3):
            terms.append(rest.astype(bf16))
            rest = rest - terms[-1].astype(f32)
        result = jnp.dot(place, jnp.concatenate(terms, axis=0), preferred_element_type=f32)
        field[...] = result.reshape(n, clusters, leaf)

    def reduce(phase, field, parts):
        send(phase, lambda peer: field.at[peer], parts)
        parts[me] = field[me]

    loads[0].wait()
    for base in range(0, far_count, 4):
        turned_right[base // 4] = right[base : base + 4].reshape(4 * rank, leaf).T
    loads[2].wait()
    for block in range(near_count):
        near[block] = near[block].T
    arrived(0, whole_p)
    pot = whole_p[...].reshape(rows, leaf)
    beta = jnp.sqrt(total(pot * pot) / panels + EPSILON)
    scale = 1.0 / beta
    product(pot * scale, field_one, True)
    reduce(1, field_one, parts_one)
    first = whole_p[...].reshape(rows, leaf) * scale
    whole_p[...] = first.reshape(n, clusters, leaf)
    g11 = total(first * first) / panels
    arrived(1, parts_one)
    mine = jnp.sum(parts_one[...], axis=0)
    middle = leaf // 2
    whole_i[me] = jnp.concatenate([mine[:, :middle], mine[:, middle:]], axis=0).astype(bf16)
    send(2, lambda peer: whole_i.at[me], whole_i)
    first = whole_p[...].reshape(rows, leaf)
    arrived(2, whole_i)
    image = whole_i[...].astype(f32)
    image = jnp.concatenate(
        [image[:, :clusters].reshape(rows, middle), image[:, clusters:].reshape(rows, middle)], axis=1
    )
    h11 = total(image * first) / panels
    squared = total(image * image) / panels + h11 * h11 * (g11 - 2.0)
    h21 = jnp.sqrt(jnp.maximum(squared, 0.0) + EPSILON)
    scale = 1.0 / h21
    second = (image - h11 * first) * scale
    product(second, field_two, False)
    reduce(3, field_two, parts_two)
    g12 = total(first * second) / panels
    g22 = total(second * second) / panels
    own_first = whole_p[me]
    own_second = (mine - h11 * own_first) * scale
    arrived(3, parts_two)
    own = jnp.sum(parts_two[...], axis=0)

    def fold(values):
        values = jnp.sum(values, axis=0, keepdims=True)
        return sum(values[:, at : at + 128] for at in range(0, leaf, 128))

    sums[me, 0:1] = fold(own * own_first)
    sums[me, 1:2] = fold(own * own_second)
    sums[me, 2:3] = fold(own * own)
    sums[me, 3:4] = jnp.zeros((1, 128), f32)
    send(4, lambda peer: sums.at[me], sums)
    arrived(4, sums)
    moments = jnp.sum(jnp.sum(sums[...], axis=0), axis=1, keepdims=True) / panels
    h12, h22, squared = moments[0:1], moments[1:2], moments[2:3]
    squared = (
        squared - 2.0 * (h12 * h12 + h22 * h22)
        + h12 * h12 * g11 + 2.0 * h12 * h22 * g12 + h22 * h22 * g22
    )
    h32 = jnp.sqrt(jnp.maximum(squared, 0.0) + EPSILON)
    krylov[0] = own_second
    krylov[1] = (own - h12 * own_first - h22 * own_second) / h32
    lane = iota(hessen.shape, 1)
    line = jnp.zeros(hessen.shape, f32)
    for position, value in enumerate([beta, h11, h21, h12, h22, h32]):
        line = jnp.where(lane == position, value, line)
    hessen[...] = line
    for phase, target in enumerate([whole_p, parts_one, whole_i, parts_two, sums]):
        sent(phase, target)


def on_device(
    potential, near_tiles, far_left, far_right, col_owner, col_local, row_owner, row_local, far_rank
):
    n = lax.axis_size("rows")
    clusters, leaf = potential.shape
    blocks = col_owner.shape[0]
    near_count = near_tiles.shape[0]
    far_count, rank = far_left.shape[:2]
    rows = n * clusters
    f32, bf16 = jnp.float32, jnp.bfloat16
    vmem = pl.BlockSpec(memory_space=pltpu.VMEM)
    anywhere = pl.BlockSpec(memory_space=pl.ANY)
    slabs = pltpu.VMEM((n, clusters, leaf), f32)
    krylov, hessen = pl.pallas_call(
        functools.partial(kernel, n),
        out_shape=(pltpu.VMEM((2, clusters, leaf), f32), pltpu.VMEM((1, 6), f32)),
        in_specs=[anywhere] * 9,
        out_specs=(vmem, vmem),
        scratch_shapes=[
            pltpu.VMEM((clusters, leaf), f32),
            pltpu.VMEM((1, blocks), jnp.int32),
            pltpu.VMEM((1, blocks), jnp.int32),
            pltpu.VMEM((1, blocks), jnp.int32),
            pltpu.VMEM((1, blocks), jnp.int32),
            pltpu.VMEM((1, far_count), jnp.int32),
            pltpu.VMEM(near_tiles.shape, bf16),
            pltpu.VMEM(far_left.shape, bf16),
            pltpu.VMEM(far_right.shape, bf16),
            pltpu.VMEM((far_count // 4, leaf, 4 * rank), bf16),
            pltpu.VMEM((far_count, 16 * rank), f32),
            slabs, slabs, slabs,
            pltpu.VMEM((n, 2 * clusters, leaf // 2), bf16),
            slabs, slabs,
            pltpu.VMEM((n, 4, 128), f32),
            pltpu.SemaphoreType.DMA((9,)),
            pltpu.SemaphoreType.DMA((5,)),
            pltpu.SemaphoreType.DMA((5,)),
        ],
        compiler_params=pltpu.CompilerParams(
            collective_id=0, has_side_effects=True, vmem_limit_bytes=56 * 1024 * 1024
        ),
        name="arnoldi",
    )(
        potential, near_tiles, far_left, far_right,
        col_owner.reshape(1, blocks), col_local.reshape(1, blocks),
        row_owner.reshape(1, blocks), row_local.reshape(1, blocks),
        far_rank.reshape(1, far_count),
    )
    return (krylov, hessen)


def solution(mesh):
    placed = (
        P(("groups", "rows"), None),
        P(("groups", "rows"), None, None),
        P(("groups", "rows"), None, None),
        P(("groups", "rows"), None, None),
        P(("groups", "rows"), None),
        P(("groups", "rows")),
        P(("groups", "rows"), None),
        P(("groups", "rows")),
        P(("groups", "rows")),
    )
    return jax.shard_map(
        on_device,
        mesh=mesh,
        in_specs=placed,
        out_specs=(P(None, ("groups", "rows"), None), P("groups", None)),
        check_vma=False,
    )
```
